512 devices in a mesh: shard: 32 (over y, x), grp: 16 (over z, core).
Axes of the slice: x: 4, y: 8, z: 8, core: 2. Of those that a mesh axis runs over, the one named last changes fastest.
Arguments:
- embeddings: bfloat16 [262144, 768], P(('shard', 'grp'))
- cluster_ids: int32 [512], P(('shard', 'grp')), may hold values from 0 to 73, as said below
Outputs:
- max_sim: float32 [262144], P(('shard', 'grp'))
- log_mass: float32 [262144], P(('shard', 'grp'))
- centroid_cos: float32 [262144], P(('shard', 'grp'))
The draws below stay inside these ranges and needn't reach their ends.
Inputs may be any that keep to these rules, and one draw needn't show every extreme that they name: `cluster_ids`: cluster ids begin at 0 on the first block, never fall along the blocks and rise by one from each cluster to the next; every cluster holds 6 to 8 consecutive blocks, and some cluster holds exactly 8.
All inputs are finite; a program needn't handle non-finite values.
Results may differ from the reference program's by a relative error of at most 0.00053.
Values may be sent and summed in bfloat16 or wider, within the bound.
No kernel may reach another device: no remote copies, remote signals or barrier semaphores. Data moves between devices by JAX's collectives and lax.ppermute only.
A program may use at most 64 MiB of HBM per device.

```python
import math
import jax
import jax.numpy as jnp
from jax import lax

D = 768
BLK = 512
CMAX = 8
NB = 512
ROWS = 262144


side_weight = 0.35


def cluster_blocks(key):
    groups = (NB + CMAX - 2) // (CMAX - 1)
    deficit = CMAX * groups - NB
    key_full, key_cuts = jax.random.split(key)
    kept_full = jax.random.randint(key_full, (), 0, groups)
    ranking = jax.random.permutation(key_cuts, 2 * (groups - 1))
    cuts = (ranking < deficit).astype(jnp.int32).reshape(groups - 1, 2).sum(axis=1)
    others = jnp.arange(groups - 1, dtype=jnp.int32)
    target = others + (others >= kept_full).astype(jnp.int32)
    shrink = jnp.zeros((groups,), jnp.int32).at[target].set(cuts)
    ends = jnp.cumsum(CMAX - shrink)
    blocks_index = jnp.arange(NB, dtype=jnp.int32)
    return jnp.sum((ends[None, :] <= blocks_index[:, None]).astype(jnp.int32), axis=1).astype(jnp.int32)


def draw_cluster_ids(key, part):
    return cluster_blocks(key)


def draw_embeddings(key, part):
    cluster_of = cluster_blocks(key)
    key = jax.random.fold_in(key, 5)
    key_centre, key_side, key_mix, key_noise, key_share = jax.random.split(key, 5)
    centres = jax.random.truncated_normal(key_centre, -4.0, 4.0, (NB, D), jnp.float32)
    sides = jax.random.truncated_normal(key_side, -4.0, 4.0, (NB, D), jnp.float32)
    mixing = jax.random.uniform(key_mix, (NB,), jnp.float32, 0.2, 0.7)
    noise = jax.random.truncated_normal(key_noise, -4.0, 4.0, (NB, BLK, D), jnp.float32)
    shares = jax.random.uniform(key_share, (NB, BLK), jnp.float32, 0.0, 0.95)
    remain = jnp.sqrt(1.0 - mixing * mixing - side_weight * side_weight)
    centre_rows = centres[cluster_of]
    base = mixing[:, None, None] * centre_rows[:, None, :] + side_weight * sides[:, None, :] + remain[:, None, None] * noise
    blocks_index = jnp.arange(NB, dtype=jnp.int32)
    first_block = jnp.min(jnp.where(cluster_of[None, :] == cluster_of[:, None], blocks_index[None, :], NB), axis=1)
    odd_place = (blocks_index - first_block) % 2 == 1
    copy_weight = jnp.where(odd_place[:, None], shares, 0.0)
    earlier = jnp.roll(base, 1, axis=0)
    mixed_rows = copy_weight[:, :, None] * earlier + jnp.sqrt(1.0 - copy_weight * copy_weight)[:, :, None] * base
    return mixed_rows.reshape(ROWS, D).astype(jnp.bfloat16)


def setup_inputs(seed: int = 0) -> dict:
    keys = jax.random.split(jax.random.key(seed), 3)
    return {
        "embeddings": draw_embeddings(jax.random.fold_in(keys[2], 71), 0),
        "cluster_ids": draw_cluster_ids(jax.random.fold_in(keys[2], 71), 0),
    }


TAU = 0.05

def unit_rows(values):
    floats = values.astype(jnp.float32)
    scale = lax.rsqrt(lax.optimization_barrier(jnp.mean(floats * floats, axis=-1, keepdims=True)) + 1e-06) / math.sqrt(floats.shape[-1])
    return (floats * scale).astype(jnp.bfloat16)

def reference(embeddings, cluster_ids):
    unit = unit_rows(embeddings)
    blocks = unit.reshape(NB, BLK, D)
    marker = (cluster_ids + 1).astype(jnp.float32)
    same = jnp.arange(BLK)[:, None] == jnp.arange(BLK)[None, :]
    row_max = jnp.full((NB, BLK), -2.0, jnp.float32)
    row_sum = jnp.zeros((NB, BLK), jnp.float32)
    for offset in range(CMAX):
        partner = jnp.concatenate([blocks[offset:], jnp.zeros((offset, BLK, D), jnp.bfloat16)], axis=0)
        pmark = jnp.concatenate([marker[offset:], jnp.zeros((offset,), jnp.float32)], axis=0)
        valid = pmark == marker

        def tile(items):
            left, right, keep = items
            sims = jnp.dot(left, right.T, preferred_element_type=jnp.float32)
            weights = jnp.exp(sims / TAU)
            if offset == 0:
                sims = jnp.where(same, -2.0, sims)
                weights = jnp.where(same, 0.0, weights)
            rmax = jnp.where(keep, lax.optimization_barrier(jnp.max(sims, axis=1)), -2.0)
            rsum = jnp.where(keep, lax.optimization_barrier(jnp.sum(weights, axis=1)), 0.0)
            cmax = jnp.where(keep, lax.optimization_barrier(jnp.max(sims, axis=0)), -2.0)
            csum = jnp.where(keep, lax.optimization_barrier(jnp.sum(weights, axis=0)), 0.0)
            return (rmax, rsum, cmax, csum)
        rmax, rsum, cmax, csum = lax.map(tile, (blocks, partner, valid))
        row_max = jnp.maximum(row_max, rmax)
        row_sum = row_sum + rsum
        if offset > 0:
            moved_max = jnp.concatenate([jnp.full((offset, BLK), -2.0, jnp.float32), cmax[:-offset]], axis=0)
            moved_sum = jnp.concatenate([jnp.zeros((offset, BLK), jnp.float32), csum[:-offset]], axis=0)
            row_max = jnp.maximum(row_max, moved_max)
            row_sum = row_sum + moved_sum
    block_sums = lax.optimization_barrier(jnp.sum(blocks.astype(jnp.float32), axis=1))
    sums = jax.ops.segment_sum(block_sums, cluster_ids, num_segments=NB)
    total = sums[cluster_ids]
    centre = total * lax.rsqrt(lax.optimization_barrier(jnp.mean(total * total, axis=-1, keepdims=True)) + 1e-06) / math.sqrt(D)
    cosines = lax.optimization_barrier(jnp.sum(blocks.astype(jnp.float32) * centre[:, None, :], axis=-1))
    return (row_max.reshape(ROWS), jnp.log(row_sum).reshape(ROWS), cosines.reshape(ROWS))
```

```python
import functools
import math

import jax
import jax.numpy as jnp
from jax import lax
from jax.experimental import pallas as pl
from jax.experimental.pallas import tpu as pltpu
from jax.sharding import PartitionSpec as P

TAU = 0.05
LOW = -2.0
TO_EXP2 = math.log2(math.e) / TAU
AXES = ("shard", "grp")
VMEM = pl.BlockSpec(memory_space=pltpu.VMEM)
F32 = jnp.float32
BF16 = jnp.bfloat16


def shape(*dims, dtype=F32):
    return jax.ShapeDtypeStruct(dims, dtype)


def call(kernel, outs, *args, flops=0, limit=24):
    single = not isinstance(outs, (list, tuple))
    size = sum(a.size * a.dtype.itemsize for a in args)
    return pl.pallas_call(
        kernel,
        out_shape=outs,
        in_specs=[VMEM] * len(args),
        out_specs=VMEM if single else [VMEM] * len(outs),
        compiler_params=pltpu.CompilerParams(vmem_limit_bytes=limit << 20),
        cost_estimate=pl.CostEstimate(flops=flops, bytes_accessed=size, transcendentals=0),
    )(*args)


def blocks_moved(value, steps, core=None, closed=False):
    count = lax.axis_size(AXES)
    sources = [i for i in range(count) if core in (None, i % 2) and (closed or 0 <= i + steps < count)]
    pairs = [(i, (i + steps) % count) for i in sources]
    return lax.ppermute(value, AXES, pairs)


def cores_swapped(value):
    return lax.ppermute(value, AXES, [(i, i ^ 1) for i in range(lax.axis_size(AXES))])


def after(value, *others):
    return lax.optimization_barrier((value, *others))[0]


def unit_kernel(emb_ref, tag_ref, unit_ref, info_ref):
    rows, width = emb_ref.shape
    floats = emb_ref[...].astype(F32)
    mean = jnp.sum(floats * floats, axis=1, keepdims=True) / width
    unit = (floats * (lax.rsqrt(mean + 1e-06) / math.sqrt(width))).astype(BF16)
    unit_ref[...] = unit
    ones = jnp.ones((8, rows), BF16)
    total = jnp.dot(ones, unit, preferred_element_type=F32)
    info_ref[0:1, :] = total[0:1, :]
    info_ref[1:2, :] = jnp.broadcast_to(tag_ref[...], (1, width))


def window_kernel(mine_ref, left_ref, here_ref, right_ref, suffix_ref, prefix_ref, window_ref):
    refs = (left_ref, here_ref, right_ref)
    sums = [ref[2 * core : 2 * core + 1, :] for ref in refs for core in range(2)]
    tags = [ref[2 * core + 1 : 2 * core + 2, :] for ref in refs for core in range(2)]

    def sum_of(tag):
        return functools.reduce(
            jnp.add, [jnp.where(other == tag, value, 0.0) for value, other in zip(sums, tags)]
        )

    suffix_ref[0:1, :] = sum_of(tags[-1])
    suffix_ref[1:2, :] = tags[-1]
    prefix_ref[0:1, :] = sum_of(tags[0])
    prefix_ref[1:2, :] = tags[0]
    prefix_ref[2:3, :] = tags[1]
    prefix_ref[3:4, :] = tags[1]
    window_ref[...] = sum_of(mine_ref[1:2, :])


def centre_kernel(mine_ref, here_ref, left_ref, window_ref, suffix_ref, prefix_ref, unit_ref, core_ref, cos_ref, flag_ref):
    rows, width = unit_ref.shape
    tag = mine_ref[1:2, :]
    total = window_ref[...]
    total += jnp.where(suffix_ref[1:2, :] == tag, suffix_ref[0:1, :], 0.0)
    total += jnp.where(prefix_ref[1:2, :] == tag, prefix_ref[0:1, :], 0.0)
    mean = jnp.sum(total * total, axis=1, keepdims=True) / width
    centre = total * (lax.rsqrt(mean + 1e-06) / math.sqrt(width))
    high = centre.astype(BF16)
    rest = centre - high.astype(F32)
    middle = rest.astype(BF16)
    low = (rest - middle.astype(F32)).astype(BF16)
    cosines = jnp.zeros((8, rows), F32)
    for part in (low, middle, high):
        cosines += lax.dot_general(
            jnp.broadcast_to(part, (8, width)), unit_ref[...], (((1,), (1,)), ((), ())), preferred_element_type=F32
        )
    cos_ref[...] = cosines[0:1, :]

    lead = slice(0, rows)
    core = core_ref[0:1, lead] > 0.5
    tag = tag[:, lead]
    pair = lambda ref, which: ref[2 * which + 1 : 2 * which + 2, lead]
    other = jnp.where(core, pair(here_ref, 0), pair(here_ref, 1))
    near = jnp.where(core, pair(left_ref, 1), pair(left_ref, 0))
    near_x = jnp.where(core, pair(left_ref, 0), pair(left_ref, 1))
    far = jnp.where(core, prefix_ref[2:3, lead], prefix_ref[1:2, lead])
    back = suffix_ref[1:2, lead]
    one = lambda same: jnp.where(same, 1.0, 0.0)
    flags = (
        one(near == tag),
        one(near == other),
        one(far == tag),
        one(far == other),
        one(far == near),
        one(far == near_x),
        jnp.where(core, one(tag == other), one(far == back)),
        one(core),
    )
    for at, flag in enumerate(flags):
        flag_ref[at : at + 1, :] = flag


def tile(left, right):
    return lax.dot_general(left, right, (((1,), (1,)), ((), ())), preferred_element_type=F32)


def lane_groups(value, combine):
    return functools.reduce(combine, [value[:, at : at + 128] for at in range(0, value.shape[1], 128)])


def rows_done(value, combine):
    return combine(value.T, axis=0, keepdims=True)


class Columns:
    def __init__(self, rows):
        self.top = jnp.full((1, rows), LOW, F32)
        self.mass = jnp.zeros((1, rows), F32)

    def add(self, top, mass, flag=None):
        if flag is not None:
            top = jnp.where(flag, top, LOW)
            mass = jnp.where(flag, mass, 0.0)
        self.top = jnp.maximum(self.top, top)
        self.mass = self.mass + mass

    def merge(self, ref, at):
        self.add(ref[at : at + 1, :], ref[at + 1 : at + 2, :])

    def store(self, ref, at):
        ref[at : at + 1, :] = self.top
        ref[at + 1 : at + 2, :] = self.mass


def strip(rows_value, others, flags, outs, out_rows):
    row_top = row_mass = None
    for other, flag, out in zip(others, flags, outs):
        sims = tile(rows_value, other)
        weights = jnp.exp2(sims * TO_EXP2)
        out.add(jnp.max(sims, axis=0, keepdims=True), jnp.sum(weights, axis=0, keepdims=True), flag)
        top = jnp.where(flag[:, :128], lane_groups(sims, jnp.maximum), LOW)
        mass = jnp.where(flag[:, :128], lane_groups(weights, jnp.add), 0.0)
        row_top = top if row_top is None else jnp.maximum(row_top, top)
        row_mass = mass if row_mass is None else row_mass + mass
    out_rows.append((rows_done(row_top, jnp.max), rows_done(row_mass, jnp.sum)))


STRIP = 256


def near_kernel(unit_ref, other_ref, near_ref, flag_ref, out_ref):
    rows = unit_ref.shape[0]
    flags = flag_ref[...] > 0.5
    unit, other = unit_ref[...], other_ref[...]
    mine, across, near = Columns(rows), Columns(rows), []
    for at in range(0, rows, STRIP):
        sims = tile(unit_ref[at : at + STRIP, :], unit)
        row = lax.broadcasted_iota(jnp.int32, sims.shape, 0) + at
        same = row == lax.broadcasted_iota(jnp.int32, sims.shape, 1)
        weights = jnp.where(same, 0.0, jnp.exp2(sims * TO_EXP2))
        sims = jnp.where(same, LOW, sims)
        mine.add(jnp.max(sims, axis=0, keepdims=True), jnp.sum(weights, axis=0, keepdims=True))
        strip(near_ref[at : at + STRIP, :], (unit, other), (flags[0:1], flags[1:2]), (mine, across), near)
    mine.store(out_ref, 0)
    across.store(out_ref, 2)
    for at, (top, mass) in enumerate(near):
        out_ref[4:5, at * STRIP : (at + 1) * STRIP] = top
        out_ref[5:6, at * STRIP : (at + 1) * STRIP] = mass
    out_ref[6:8, :] = jnp.zeros((2, rows), F32)


def far_kernel(far_ref, unit_ref, other_ref, near_ref, near_x_ref, flag_ref, out_ref):
    rows = unit_ref.shape[0]
    flags = flag_ref[...] > 0.5
    columns = [Columns(rows) for _ in range(4)]
    far = []
    blocks = (unit_ref[...], other_ref[...], near_ref[...], near_x_ref[...])
    strip(far_ref[...], blocks, [flags[at : at + 1] for at in range(2, 6)], columns, far)
    for at, column in enumerate(columns):
        column.store(out_ref, 2 * at)
    count = far_ref.shape[0]
    out_ref[8:9, :count] = far[0][0]
    out_ref[9:10, :count] = far[0][1]
    out_ref[8:10, count:] = jnp.zeros((2, rows - count), F32)
    out_ref[10:16, :] = jnp.zeros((6, rows), F32)


def last_kernel(
    far_a_ref, far_b_ref, unit_ref, other_ref, near_ref, near_x_ref, back_ref, flag_ref, stats_near_ref, stats_far_ref,
    mine_ref, swap_ref, near_out_ref, far_out_ref, back_out_ref,
):
    rows = unit_ref.shape[0]
    flags = flag_ref[...] > 0.5
    mine, across, near, near_x = columns = [Columns(rows) for _ in range(4)]
    far = [(stats_far_ref[8:9, :STRIP], stats_far_ref[9:10, :STRIP])]
    blocks = (unit_ref[...], other_ref[...], near_ref[...], near_x_ref[...])
    strip(far_b_ref[...], blocks, [flags[at : at + 1] for at in range(2, 6)], columns, far)
    second = jnp.max(flag_ref[7:8, 0:1]) > 0.5
    flag = flags[6:7]
    last, extra = Columns(rows), []
    rows_a = jnp.where(second, unit_ref[:STRIP, :], far_a_ref[...])
    rows_b = jnp.where(second, unit_ref[STRIP:, :], far_b_ref[...])
    block = jnp.where(second, other_ref[...], back_ref[...])
    for value in (rows_a, rows_b):
        strip(value, (block,), (flag,), (last,), extra)
    none = Columns(rows)
    whole = lambda parts: [jnp.concatenate([part[which] for part in parts], axis=1) for which in range(2)]
    extra, far = whole(extra), whole(far)
    core = flags[7:8]
    mine.add(extra[0], extra[1], core)
    across.add(last.top, last.mass, core)
    far_top = jnp.maximum(far[0], jnp.where(core, LOW, extra[0]))
    far_mass = far[1] + jnp.where(core, 0.0, extra[1])
    none.add(last.top, last.mass, jnp.logical_not(core))
    mine.merge(stats_near_ref, 0)
    mine.merge(stats_far_ref, 0)
    across.merge(stats_near_ref, 2)
    across.merge(stats_far_ref, 2)
    near.merge(stats_near_ref, 4)
    near.merge(stats_far_ref, 4)
    near_x.merge(stats_far_ref, 6)
    mine.store(mine_ref, 0)
    across.store(swap_ref, 0)
    near_x.store(swap_ref, 2)
    near.store(near_out_ref, 0)
    far_out_ref[0:1, :] = far_top
    far_out_ref[1:2, :] = far_mass
    none.store(back_out_ref, 0)


def merged(columns, ref, at):
    mass = ref[at + 1 : at + 2, :]
    columns.add(ref[at : at + 1, :], mass, mass > 0.0)


def near_sum_kernel(near_ref, swap_ref, out_ref):
    near = Columns(near_ref.shape[1])
    near.merge(near_ref, 0)
    near.merge(swap_ref, 2)
    near.store(out_ref, 0)


def final_kernel(mine_ref, swap_ref, far_ref, back_ref, near_ref, top_ref, log_ref):
    mine = Columns(mine_ref.shape[1])
    mine.merge(mine_ref, 0)
    for ref in (swap_ref, far_ref, back_ref, near_ref):
        merged(mine, ref, 0)
    top_ref[...] = mine.top
    log_ref[...] = jnp.log(mine.mass)


def per_device(embeddings, cluster_ids):
    rows, width = embeddings.shape
    tile_flops = 2 * rows * rows * width
    core = lax.axis_index("grp") % 2
    tag = (cluster_ids + 1).astype(F32).reshape(1, 1)
    unit, info = call(unit_kernel, [shape(rows, width, dtype=BF16), shape(2, width)], embeddings, tag)

    near = blocks_moved(unit, 2)
    far_a = blocks_moved(unit[:STRIP], -4)
    info_x = cores_swapped(info)
    other = cores_swapped(unit)
    pair = jnp.where(core == 0, jnp.concatenate([info, info_x]), jnp.concatenate([info_x, info]))
    pair_left = blocks_moved(pair, 2, closed=True)
    pair_right = blocks_moved(pair, -2, closed=True)
    suffix, prefix, window = call(
        window_kernel, [shape(2, width), shape(4, width), shape(1, width)], info, pair_left, pair, pair_right
    )
    left_suffix = blocks_moved(suffix, 6, closed=True)
    right_prefix = blocks_moved(prefix, -6, closed=True)
    far_b = blocks_moved(after(unit[STRIP:], near), -4)
    near_x = cores_swapped(near)
    back = blocks_moved(after(unit, near), 3, core=1)
    cores = jnp.full((1, rows), core, F32)
    cosines, flags = call(
        centre_kernel,
        [shape(1, rows), shape(8, rows)],
        info, pair, pair_left, window, left_suffix, right_prefix, unit, cores,
    )
    stats_near = call(near_kernel, shape(8, rows), unit, other, near, flags, flops=3 * tile_flops)
    stats_far = call(far_kernel, shape(16, rows), far_a, unit, other, near, near_x, flags, flops=2 * tile_flops)
    mine, swap, near_out, far_out, back_out = call(
        last_kernel,
        [shape(2, rows), shape(4, rows), shape(2, rows), shape(2, rows), shape(2, rows)],
        far_a, far_b, unit, other, near, near_x, back, flags, stats_near, stats_far,
        flops=3 * tile_flops,
    )
    swap_in = cores_swapped(swap)
    far_in = blocks_moved(far_out, 4)
    back_in = blocks_moved(back_out, -3, core=0)
    near_in = blocks_moved(call(near_sum_kernel, shape(2, rows), near_out, swap_in), -2)
    top, log_mass = call(final_kernel, [shape(1, rows), shape(1, rows)], mine, swap_in, far_in, back_in, near_in)
    return top.reshape(rows), log_mass.reshape(rows), cosines.reshape(rows)


def solution(mesh):
    in_specs = (P(AXES, None), P(AXES))
    out_specs = (P(AXES), P(AXES), P(AXES))
    return jax.shard_map(per_device, mesh=mesh, in_specs=in_specs, out_specs=out_specs, check_vma=False)
```

```python
import functools
import math

import jax
import jax.numpy as jnp
from jax import lax
from jax.experimental import pallas as pl
from jax.experimental.pallas import tpu as pltpu
from jax.sharding import PartitionSpec as P

TAU = 0.05
LOW = -2.0
TO_EXP2 = math.log2(math.e) / TAU
AXES = ("shard", "grp")
VMEM = pl.BlockSpec(memory_space=pltpu.VMEM)
F32 = jnp.float32
BF16 = jnp.bfloat16
LANES = 128
TAIL = 16
STRIP = 256


def shape(*dims, dtype=F32):
    return jax.ShapeDtypeStruct(dims, dtype)


def call(kernel, outs, *args, flops=0, limit=16):
    single = not isinstance(outs, (list, tuple))
    size = sum(a.size * a.dtype.itemsize for a in args)
    return pl.pallas_call(
        kernel,
        out_shape=outs,
        in_specs=[VMEM] * len(args),
        out_specs=VMEM if single else [VMEM] * len(outs),
        compiler_params=pltpu.CompilerParams(vmem_limit_bytes=limit << 20),
        cost_estimate=pl.CostEstimate(flops=flops, bytes_accessed=size, transcendentals=0),
    )(*args)


def blocks_moved(value, steps, core=None):
    count = lax.axis_size(AXES)
    pairs = [(i, i + steps) for i in range(count) if core in (None, i % 2) and 0 <= i + steps < count]
    return lax.ppermute(value, AXES, pairs)


def cores_swapped(value):
    return lax.ppermute(value, AXES, [(i, i ^ 1) for i in range(lax.axis_size(AXES))])


def after(value, *others):
    return lax.optimization_barrier((value, *others))[0]


def parts_of(value):
    high = value.astype(BF16)
    rest = value - high.astype(F32)
    middle = rest.astype(BF16)
    return high, middle, (rest - middle.astype(F32)).astype(BF16)


def unit_kernel(id_ref, emb_ref, block_ref):
    rows, width = emb_ref.shape
    total = jnp.zeros((8, width), F32)
    for at in range(0, rows, STRIP // 2):
        strip_rows = slice(at, at + STRIP // 2)
        floats = emb_ref[strip_rows, :].astype(F32)
        mean = jnp.sum(floats * floats, axis=1, keepdims=True) / width
        unit = (floats * (lax.rsqrt(mean + 1e-06) / math.sqrt(width))).astype(BF16)
        block_ref[strip_rows, :] = unit
        total += jnp.dot(jnp.ones((8, STRIP // 2), BF16), unit, preferred_element_type=F32)
    parts = [part.astype(F32) for part in parts_of(total[0:1, :])]
    tag = jnp.full((1, width), (id_ref[0] + 1).astype(F32))
    block_ref[rows:, :] = jnp.concatenate(parts + [tag, jnp.zeros((TAIL - 4, width), F32)]).astype(BF16)


def unit_block(embeddings, cluster_ids):
    rows, width = embeddings.shape
    return pl.pallas_call(
        unit_kernel,
        out_shape=shape(rows + TAIL, width, dtype=BF16),
        in_specs=[pl.BlockSpec(memory_space=pltpu.SMEM), VMEM],
        out_specs=VMEM,
        compiler_params=pltpu.CompilerParams(vmem_limit_bytes=16 << 20),
    )(cluster_ids, embeddings)


def this_core():
    return lax.rem(lax.axis_index("grp"), 2)


def rows_of(ref):
    return ref[: ref.shape[0] - TAIL, :]


def tail_of(ref):
    tail = ref[ref.shape[0] - TAIL :, :].astype(F32)
    return tail[0:1, :] + (tail[1:2, :] + tail[2:3, :]), tail[3:4, :]


def tile(left, right):
    return lax.dot_general(left, right, (((1,), (1,)), ((), ())), preferred_element_type=F32)


def lane_groups(value, combine):
    return functools.reduce(combine, [value[:, at : at + 128] for at in range(0, value.shape[1], 128)])


def rows_done(value, combine):
    return combine(value.T, axis=0, keepdims=True)


class Columns:
    def __init__(self, rows, width=0):
        self.top = jnp.full((1, rows), LOW, F32)
        self.mass = jnp.zeros((1, rows), F32)
        self.total = jnp.zeros((1, width), F32)

    def add(self, top, mass, flag=None):
        if flag is not None:
            top = jnp.where(flag, top, LOW)
            mass = jnp.where(flag, mass, 0.0)
        self.top = jnp.maximum(self.top, top)
        self.mass = self.mass + mass

    def meet(self, total, flag=None):
        self.total = self.total + (total if flag is None else jnp.where(flag, total, 0.0))

    def load(self, ref, at):
        rows = self.top.shape[1]
        self.add(ref[at : at + 1, :rows], ref[at + 1 : at + 2, :rows])

    def store(self, ref, at):
        rows = self.top.shape[1]
        ref[at : at + 1, :rows] = self.top
        ref[at + 1 : at + 2, :rows] = self.mass
        if self.total.size:
            ref[at : at + 2, rows:] = jnp.zeros((2, ref.shape[1] - rows), F32)
            ref[at + 2 : at + 3, :] = self.total

    def receive(self, ref, at):
        rows = self.top.shape[1]
        mass = ref[at + 1 : at + 2, :rows]
        self.add(ref[at : at + 1, :rows], mass, mass > 0.0)
        self.meet(ref[at + 2 : at + 3, :])


def strip(rows_value, others, flags, outs, out_rows):
    row_top = row_mass = None
    for other, flag, out in zip(others, flags, outs):
        sims = tile(rows_value, other)
        weights = jnp.exp2(sims * TO_EXP2)
        out.add(jnp.max(sims, axis=0, keepdims=True), jnp.sum(weights, axis=0, keepdims=True), flag[:, : sims.shape[1]])
        top = jnp.where(flag[:, :LANES], lane_groups(sims, jnp.maximum), LOW)
        mass = jnp.where(flag[:, :LANES], lane_groups(weights, jnp.add), 0.0)
        row_top = top if row_top is None else jnp.maximum(row_top, top)
        row_mass = mass if row_mass is None else row_mass + mass
    out_rows.append((rows_done(row_top, jnp.max), rows_done(row_mass, jnp.sum)))


def whole(parts):
    return [jnp.concatenate([part[which] for part in parts], axis=1) for which in range(2)]


def near_kernel(unit_ref, other_ref, near_ref, out_ref):
    unit, other = rows_of(unit_ref), rows_of(other_ref)
    rows = unit.shape[0]
    (_, tag), (_, tag_other), (_, tag_near) = [tail_of(ref) for ref in (unit_ref, other_ref, near_ref)]
    mine, across, near, parts = Columns(rows), Columns(rows), Columns(rows), []
    for at in range(0, rows, STRIP):
        sims = tile(unit_ref[at : at + STRIP, :], unit)
        row = lax.broadcasted_iota(jnp.int32, sims.shape, 0) + at
        same = row == lax.broadcasted_iota(jnp.int32, sims.shape, 1)
        weights = jnp.where(same, 0.0, jnp.exp2(sims * TO_EXP2))
        sims = jnp.where(same, LOW, sims)
        mine.add(jnp.max(sims, axis=0, keepdims=True), jnp.sum(weights, axis=0, keepdims=True))
        strip(near_ref[at : at + STRIP, :], (unit, other), (tag_near == tag, tag_near == tag_other), (mine, across), parts)
    near.add(*whole(parts))
    for at, columns in ((0, mine), (2, across), (4, near)):
        columns.store(out_ref, at)
    out_ref[6:8, :] = jnp.zeros((2, rows), F32)


def far_kernel(
    far_ref, unit_ref, other_ref, near_ref, near_x_ref, back_ref, stats_ref,
    mine_ref, swap_ref, near_out_ref, far_out_ref, back_out_ref,
):
    unit, other = rows_of(unit_ref), rows_of(other_ref)
    rows, width = unit.shape
    second = this_core() == 1
    mine, across, near, near_x = columns = [Columns(rows, width) for _ in range(4)]
    theirs, beyond, last = Columns(rows, width), Columns(rows, width), Columns(rows)
    blocks = (unit, other, rows_of(near_ref), rows_of(near_x_ref))
    tails = [tail_of(ref) for ref in (unit_ref, other_ref, near_ref, near_x_ref)]
    far_tail, back_tail = tail_of(far_ref), tail_of(back_ref)
    last_block = jnp.where(second, other, rows_of(back_ref))
    last_flag = jnp.where(second, tails[0][1], far_tail[1]) == jnp.where(second, tails[1][1], back_tail[1])
    flags = [tag == far_tail[1] for _, tag in tails]
    far, extra = [], []
    for at in range(0, rows, STRIP):
        far_rows = far_ref[at : at + STRIP, :]
        strip(far_rows, blocks, flags, columns, far)
        last_rows = jnp.where(second, unit_ref[at : at + STRIP, :], far_rows)
        strip(last_rows, (last_block,), (last_flag,), (last,), extra)
    mine.meet(tails[0][0])
    for (total, tag), owner in zip(tails[:2], (mine, across)):
        near.meet(total, tag == tails[2][1])
        owner.meet(tails[2][0], tag == tails[2][1])
    for (total, _), flag, owner in zip(tails, flags, columns):
        theirs.meet(total, flag)
        owner.meet(far_tail[0], flag)
    on = jnp.logical_and(last_flag, second)
    off = jnp.logical_and(last_flag, jnp.logical_not(second))
    across.meet(tails[0][0], on)
    mine.meet(tails[1][0], on)
    beyond.meet(far_tail[0], off)
    theirs.meet(back_tail[0], off)
    extra = whole(extra)
    theirs.add(*whole(far))
    theirs.add(*extra, off[:, :rows])
    mine.add(*extra, on[:, :rows])
    across.add(last.top, last.mass, on[:, :rows])
    beyond.add(last.top, last.mass, off[:, :rows])
    mine.load(stats_ref, 0)
    across.load(stats_ref, 2)
    near.load(stats_ref, 4)
    mine.store(mine_ref, 0)
    across.store(swap_ref, 0)
    near_x.store(swap_ref, 3)
    near.store(near_out_ref, 0)
    theirs.store(far_out_ref, 0)
    beyond.store(back_out_ref, 0)


def near_sum_kernel(near_ref, swap_ref, out_ref, *, rows):
    near = Columns(rows, near_ref.shape[1])
    near.receive(near_ref, 0)
    near.receive(swap_ref, 3)
    near.store(out_ref, 0)


def final_kernel(unit_ref, mine_ref, swap_ref, far_ref, back_ref, near_ref, top_ref, log_ref, cos_ref):
    unit = rows_of(unit_ref)
    rows, width = unit.shape
    mine = Columns(rows, width)
    for ref in (mine_ref, swap_ref, far_ref, back_ref, near_ref):
        mine.receive(ref, 0)
    top_ref[...] = mine.top
    log_ref[...] = jnp.log(mine.mass)
    mean = jnp.sum(mine.total * mine.total, axis=1, keepdims=True) / width
    centre = mine.total * (lax.rsqrt(mean + 1e-06) / math.sqrt(width))
    cosines = jnp.zeros((8, rows), F32)
    for part in parts_of(centre)[::-1]:
        cosines += tile(jnp.broadcast_to(part, (8, width)), unit)
    cos_ref[...] = cosines[0:1, :]


def per_device(embeddings, cluster_ids):
    rows, width = embeddings.shape
    block = unit_block(embeddings, cluster_ids)

    near = blocks_moved(block, 2)
    far = blocks_moved(block, -4)
    other = cores_swapped(block)
    back = blocks_moved(near, 1, core=1)
    near_x = cores_swapped(near)
    stats = call(near_kernel, shape(8, rows), block, other, near)
    mine, swap, near_out, far_out, back_out = call(
        far_kernel,
        [shape(3, width), shape(6, width), shape(3, width), shape(3, width), shape(3, width)],
        far, block, other, near, near_x, back, stats,
    )
    swap_in = cores_swapped(swap)
    far_in = blocks_moved(far_out, 4)
    back_in = blocks_moved(back_out, -3, core=0)
    near_all = call(functools.partial(near_sum_kernel, rows=rows), shape(3, width), near_out, swap_in)
    near_in = blocks_moved(near_all, -2)
    outs = call(final_kernel, [shape(1, rows)] * 3, block, mine, swap_in, far_in, back_in, near_in)
    return tuple(out.reshape(rows) for out in outs)


def solution(mesh):
    in_specs = (P(AXES, None), P(AXES))
    out_specs = (P(AXES), P(AXES), P(AXES))
    return jax.shard_map(per_device, mesh=mesh, in_specs=in_specs, out_specs=out_specs, check_vma=False)
```

```python
import functools
import math

import jax
import jax.numpy as jnp
from jax import lax
from jax.experimental import pallas as pl
from jax.experimental.pallas import tpu as pltpu
from jax.sharding import PartitionSpec as P

TAU = 0.05
LOW = -2.0
TO_EXP2 = math.log2(math.e) / TAU
AXES = ("shard", "grp")
VMEM = pl.BlockSpec(memory_space=pltpu.VMEM)
F32 = jnp.float32
BF16 = jnp.bfloat16
LANES = 128
TAIL = 16
STRIP = 256


def shape(*dims, dtype=F32):
    return jax.ShapeDtypeStruct(dims, dtype)


def call(kernel, outs, *args, limit=16):
    single = not isinstance(outs, (list, tuple))
    size = sum(a.size * a.dtype.itemsize for a in args)
    return pl.pallas_call(
        kernel,
        out_shape=outs,
        in_specs=[VMEM] * len(args),
        out_specs=VMEM if single else [VMEM] * len(outs),
        compiler_params=pltpu.CompilerParams(vmem_limit_bytes=limit << 20),
        cost_estimate=pl.CostEstimate(flops=0, bytes_accessed=size, transcendentals=0),
    )(*args)


def blocks_moved(value, steps, core=None):
    count = lax.axis_size(AXES)
    pairs = [(i, i + steps) for i in range(count) if core in (None, i % 2) and 0 <= i + steps < count]
    return lax.ppermute(value, AXES, pairs)


def cores_swapped(value):
    return lax.ppermute(value, AXES, [(i, i ^ 1) for i in range(lax.axis_size(AXES))])


def after(value, *others):
    return lax.optimization_barrier((value, *others))[0]


def parts_of(value):
    high = value.astype(BF16)
    rest = value - high.astype(F32)
    middle = rest.astype(BF16)
    return high, middle, (rest - middle.astype(F32)).astype(BF16)


def unit_kernel(id_ref, emb_ref, block_ref):
    rows, width = emb_ref.shape
    total = jnp.zeros((8, width), F32)
    for at in range(0, rows, STRIP // 2):
        strip_rows = slice(at, at + STRIP // 2)
        floats = emb_ref[strip_rows, :].astype(F32)
        mean = jnp.sum(floats * floats, axis=1, keepdims=True) / width
        unit = (floats * (lax.rsqrt(mean + 1e-06) / math.sqrt(width))).astype(BF16)
        block_ref[strip_rows, :] = unit
        total += jnp.dot(jnp.ones((8, STRIP // 2), BF16), unit, preferred_element_type=F32)
    parts = [part.astype(F32) for part in parts_of(total[0:1, :])]
    tag = jnp.full((1, width), (id_ref[0] + 1).astype(F32))
    block_ref[rows:, :] = jnp.concatenate(parts + [tag, jnp.zeros((TAIL - 4, width), F32)]).astype(BF16)


def unit_block(embeddings, cluster_ids):
    rows, width = embeddings.shape
    return pl.pallas_call(
        unit_kernel,
        out_shape=shape(rows + TAIL, width, dtype=BF16),
        in_specs=[pl.BlockSpec(memory_space=pltpu.SMEM), VMEM],
        out_specs=VMEM,
        compiler_params=pltpu.CompilerParams(vmem_limit_bytes=16 << 20),
    )(cluster_ids, embeddings)


def this_core():
    return lax.rem(lax.axis_index("grp"), 2)


def rows_of(ref):
    return ref[: ref.shape[0] - TAIL, :]


def tail_of(ref):
    tail = ref[ref.shape[0] - TAIL :, :].astype(F32)
    return tail[0:1, :] + (tail[1:2, :] + tail[2:3, :]), tail[3:4, :]


def tile(left, right):
    return lax.dot_general(left, right, (((1,), (1,)), ((), ())), preferred_element_type=F32)


def lane_groups(value, combine):
    return functools.reduce(combine, [value[:, at : at + 128] for at in range(0, value.shape[1], 128)])


def rows_done(value, combine):
    return combine(value.T, axis=0, keepdims=True)


class Columns:
    def __init__(self, rows, width=0):
        self.top = jnp.full((1, rows), LOW, F32)
        self.mass = jnp.zeros((1, rows), F32)
        self.total = jnp.zeros((1, width), F32)

    def add(self, top, mass, flag=None):
        if flag is not None:
            top = jnp.where(flag, top, LOW)
            mass = jnp.where(flag, mass, 0.0)
        self.top = jnp.maximum(self.top, top)
        self.mass = self.mass + mass

    def meet(self, total, flag=None):
        self.total = self.total + (total if flag is None else jnp.where(flag, total, 0.0))

    def load(self, ref, at):
        rows = self.top.shape[1]
        self.add(ref[at : at + 1, :rows], ref[at + 1 : at + 2, :rows])

    def store(self, ref, at):
        rows = self.top.shape[1]
        ref[at : at + 1, :rows] = self.top
        ref[at + 1 : at + 2, :rows] = self.mass
        if self.total.size:
            ref[at : at + 2, rows:] = jnp.zeros((2, ref.shape[1] - rows), F32)
            ref[at + 2 : at + 3, :] = self.total

    def receive(self, ref, at):
        rows = self.top.shape[1]
        mass = ref[at + 1 : at + 2, :rows]
        self.add(ref[at : at + 1, :rows], mass, mass > 0.0)
        self.meet(ref[at + 2 : at + 3, :])


def strip(rows_value, others, flags, outs, out_rows):
    row_top = row_mass = None
    for other, flag, out in zip(others, flags, outs):
        sims = tile(rows_value, other)
        weights = jnp.exp2(sims * TO_EXP2)
        out.add(jnp.max(sims, axis=0, keepdims=True), jnp.sum(weights, axis=0, keepdims=True), flag[:, : sims.shape[1]])
        top = jnp.where(flag[:, :LANES], lane_groups(sims, jnp.maximum), LOW)
        mass = jnp.where(flag[:, :LANES], lane_groups(weights, jnp.add), 0.0)
        row_top = top if row_top is None else jnp.maximum(row_top, top)
        row_mass = mass if row_mass is None else row_mass + mass
    out_rows.append((rows_done(row_top, jnp.max), rows_done(row_mass, jnp.sum)))


def whole(parts):
    return [jnp.concatenate([part[which] for part in parts], axis=1) for which in range(2)]


def near_kernel(unit_ref, near_ref, out_ref):
    unit = rows_of(unit_ref)
    rows = unit.shape[0]
    flag = tail_of(unit_ref)[1] == tail_of(near_ref)[1]
    mine, near, parts = Columns(rows), Columns(rows), []
    for at in range(0, rows, STRIP):
        sims = tile(unit_ref[at : at + STRIP, :], unit)
        row = lax.broadcasted_iota(jnp.int32, sims.shape, 0) + at
        same = row == lax.broadcasted_iota(jnp.int32, sims.shape, 1)
        weights = jnp.where(same, 0.0, jnp.exp2(sims * TO_EXP2))
        sims = jnp.where(same, LOW, sims)
        mine.add(jnp.max(sims, axis=0, keepdims=True), jnp.sum(weights, axis=0, keepdims=True))
        strip(near_ref[at : at + STRIP, :], (unit,), (flag,), (mine,), parts)
    near.add(*whole(parts))
    mine.store(out_ref, 0)
    near.store(out_ref, 2)


def far_kernel(
    far_ref, unit_ref, other_ref, near_ref, near_x_ref, back_ref, stats_ref,
    mine_ref, swap_ref, near_out_ref, far_out_ref, back_out_ref,
):
    unit, other = rows_of(unit_ref), rows_of(other_ref)
    rows, width = unit.shape
    second = this_core() == 1
    mine, across, near, near_x = columns = [Columns(rows, width) for _ in range(4)]
    theirs, beyond, last = Columns(rows, width), Columns(rows, width), Columns(rows)
    blocks = (unit, other, rows_of(near_ref), rows_of(near_x_ref))
    tails = [tail_of(ref) for ref in (unit_ref, other_ref, near_ref, near_x_ref)]
    far_tail, back_tail = tail_of(far_ref), tail_of(back_ref)
    last_block = jnp.where(second, other, rows_of(back_ref))
    last_flag = jnp.where(second, tails[0][1], far_tail[1]) == jnp.where(second, tails[1][1], back_tail[1])
    flags = [tag == far_tail[1] for _, tag in tails]
    near_flag = tails[1][1] == tails[2][1]
    far, extra, back_by = [], [], []
    for at in range(0, rows, STRIP):
        far_rows = far_ref[at : at + STRIP, :]
        strip(far_rows, blocks, flags, columns, far)
        strip(near_ref[at : at + STRIP, :], (other,), (near_flag,), (across,), back_by)
        last_rows = jnp.where(second, unit_ref[at : at + STRIP, :], far_rows)
        strip(last_rows, (last_block,), (last_flag,), (last,), extra)
    mine.meet(tails[0][0])
    for (total, tag), owner in zip(tails[:2], (mine, across)):
        near.meet(total, tag == tails[2][1])
        owner.meet(tails[2][0], tag == tails[2][1])
    for (total, _), flag, owner in zip(tails, flags, columns):
        theirs.meet(total, flag)
        owner.meet(far_tail[0], flag)
    on = jnp.logical_and(last_flag, second)
    off = jnp.logical_and(last_flag, jnp.logical_not(second))
    across.meet(tails[0][0], on)
    mine.meet(tails[1][0], on)
    beyond.meet(far_tail[0], off)
    theirs.meet(back_tail[0], off)
    extra = whole(extra)
    theirs.add(*whole(far))
    theirs.add(*extra, off[:, :rows])
    mine.add(*extra, on[:, :rows])
    across.add(last.top, last.mass, on[:, :rows])
    beyond.add(last.top, last.mass, off[:, :rows])
    near.add(*whole(back_by))
    mine.load(stats_ref, 0)
    near.load(stats_ref, 2)
    mine.store(mine_ref, 0)
    across.store(swap_ref, 0)
    near_x.store(swap_ref, 3)
    near.store(near_out_ref, 0)
    theirs.store(far_out_ref, 0)
    beyond.store(back_out_ref, 0)


def near_sum_kernel(near_ref, swap_ref, out_ref, *, rows):
    near = Columns(rows, near_ref.shape[1])
    near.receive(near_ref, 0)
    near.receive(swap_ref, 3)
    near.store(out_ref, 0)


def final_kernel(unit_ref, mine_ref, swap_ref, far_ref, back_ref, near_ref, top_ref, log_ref, cos_ref):
    unit = rows_of(unit_ref)
    rows, width = unit.shape
    mine = Columns(rows, width)
    for ref in (mine_ref, swap_ref, far_ref, back_ref, near_ref):
        mine.receive(ref, 0)
    top_ref[...] = mine.top
    log_ref[...] = jnp.log(mine.mass)
    mean = jnp.sum(mine.total * mine.total, axis=1, keepdims=True) / width
    centre = mine.total * (lax.rsqrt(mean + 1e-06) / math.sqrt(width))
    parts = [part.astype(F32) for part in parts_of(centre)]
    cosines = tile(jnp.concatenate(parts + [jnp.zeros((5, width), F32)]).astype(BF16), unit)
    cos_ref[...] = cosines[0:1, :] + (cosines[1:2, :] + cosines[2:3, :])


def per_device(embeddings, cluster_ids):
    rows, width = embeddings.shape
    block = unit_block(embeddings, cluster_ids)

    near = blocks_moved(block, 2)
    far = blocks_moved(block, -4)
    back = blocks_moved(near, 1, core=1)
    near_x = cores_swapped(near)
    other = cores_swapped(after(block, near))
    stats = call(near_kernel, shape(4, rows), block, near)
    mine, swap, near_out, far_out, back_out = call(
        far_kernel,
        [shape(3, width), shape(6, width), shape(3, width), shape(3, width), shape(3, width)],
        far, block, other, near, near_x, back, stats,
    )
    swap_in = cores_swapped(swap)
    far_in = blocks_moved(far_out, 4)
    back_in = blocks_moved(back_out, -3, core=0)
    near_all = call(functools.partial(near_sum_kernel, rows=rows), shape(3, width), near_out, swap_in)
    near_in = blocks_moved(near_all, -2)
    outs = call(final_kernel, [shape(1, rows)] * 3, block, mine, swap_in, far_in, back_in, near_in)
    return tuple(out.reshape(rows) for out in outs)


def solution(mesh):
    in_specs = (P(AXES, None), P(AXES))
    out_specs = (P(AXES), P(AXES), P(AXES))
    return jax.shard_map(per_device, mesh=mesh, in_specs=in_specs, out_specs=out_specs, check_vma=False)
```

```python
import functools
import math

import jax
import jax.numpy as jnp
from jax import lax
from jax.experimental import pallas as pl
from jax.experimental.pallas import tpu as pltpu
from jax.sharding import PartitionSpec as P

TAU = 0.05
LOW = -2.0
TO_EXP2 = math.log2(math.e) / TAU
AXES = ("shard", "grp")
VMEM = pl.BlockSpec(memory_space=pltpu.VMEM)
F32 = jnp.float32
BF16 = jnp.bfloat16
LANES = 128
TAIL = 16
STRIP = 256


def shape(*dims, dtype=F32):
    return jax.ShapeDtypeStruct(dims, dtype)


def call(kernel, outs, *args, limit=16):
    single = not isinstance(outs, (list, tuple))
    size = sum(a.size * a.dtype.itemsize for a in args)
    return pl.pallas_call(
        kernel,
        out_shape=outs,
        in_specs=[VMEM] * len(args),
        out_specs=VMEM if single else [VMEM] * len(outs),
        compiler_params=pltpu.CompilerParams(vmem_limit_bytes=limit << 20),
        cost_estimate=pl.CostEstimate(flops=0, bytes_accessed=size, transcendentals=0),
    )(*args)


def blocks_moved(value, steps, core=None):
    count = lax.axis_size(AXES)
    pairs = [(i, i + steps) for i in range(count) if core in (None, i % 2) and 0 <= i + steps < count]
    return lax.ppermute(value, AXES, pairs)


def cores_swapped(value):
    return lax.ppermute(value, AXES, [(i, i ^ 1) for i in range(lax.axis_size(AXES))])


def after(value, *others):
    return lax.optimization_barrier((value, *others))[0]


def parts_of(value):
    high = value.astype(BF16)
    rest = value - high.astype(F32)
    middle = rest.astype(BF16)
    return high, middle, (rest - middle.astype(F32)).astype(BF16)


def unit_kernel(id_ref, emb_ref, block_ref):
    rows, width = emb_ref.shape
    total = jnp.zeros((8, width), F32)
    for at in range(0, rows, STRIP // 2):
        strip_rows = slice(at, at + STRIP // 2)
        floats = emb_ref[strip_rows, :].astype(F32)
        mean = jnp.sum(floats * floats, axis=1, keepdims=True) / width
        unit = (floats * (lax.rsqrt(mean + 1e-06) / math.sqrt(width))).astype(BF16)
        block_ref[strip_rows, :] = unit
        total += jnp.dot(jnp.ones((8, STRIP // 2), BF16), unit, preferred_element_type=F32)
    parts = [part.astype(F32) for part in parts_of(total[0:1, :])]
    tag = jnp.full((1, width), (id_ref[0] + 1).astype(F32))
    block_ref[rows:, :] = jnp.concatenate(parts + [tag, jnp.zeros((TAIL - 4, width), F32)]).astype(BF16)


def unit_block(embeddings, cluster_ids):
    rows, width = embeddings.shape
    return pl.pallas_call(
        unit_kernel,
        out_shape=shape(rows + TAIL, width, dtype=BF16),
        in_specs=[pl.BlockSpec(memory_space=pltpu.SMEM), VMEM],
        out_specs=VMEM,
        compiler_params=pltpu.CompilerParams(vmem_limit_bytes=16 << 20),
    )(cluster_ids, embeddings)


def this_core():
    return lax.rem(lax.axis_index("grp"), 2)


def rows_of(ref):
    return ref[: ref.shape[0] - TAIL, :]


def tail_of(ref):
    tail = ref[ref.shape[0] - TAIL :, :].astype(F32)
    return tail[0:1, :] + (tail[1:2, :] + tail[2:3, :]), tail[3:4, :]


def tile(left, right):
    return lax.dot_general(left, right, (((1,), (1,)), ((), ())), preferred_element_type=F32)


def lane_groups(value, combine):
    return functools.reduce(combine, [value[:, at : at + 128] for at in range(0, value.shape[1], 128)])


def rows_done(value, combine):
    return combine(value.T, axis=0, keepdims=True)


class Columns:
    def __init__(self, rows, width=0):
        self.top = jnp.full((1, rows), LOW, F32)
        self.mass = jnp.zeros((1, rows), F32)
        self.total = jnp.zeros((1, width), F32)

    def add(self, top, mass, flag=None):
        if flag is not None:
            top = jnp.where(flag, top, LOW)
            mass = jnp.where(flag, mass, 0.0)
        self.top = jnp.maximum(self.top, top)
        self.mass = self.mass + mass

    def meet(self, total, flag=None):
        self.total = self.total + (total if flag is None else jnp.where(flag, total, 0.0))

    def load(self, ref, at):
        rows = self.top.shape[1]
        self.add(ref[at : at + 1, :rows], ref[at + 1 : at + 2, :rows])

    def store(self, ref, at):
        rows = self.top.shape[1]
        ref[at : at + 1, :rows] = self.top
        ref[at + 1 : at + 2, :rows] = self.mass
        if self.total.size:
            ref[at : at + 2, rows:] = jnp.zeros((2, ref.shape[1] - rows), F32)
            ref[at + 2 : at + 3, :] = self.total

    def receive(self, ref, at):
        rows = self.top.shape[1]
        mass = ref[at + 1 : at + 2, :rows]
        self.add(ref[at : at + 1, :rows], mass, mass > 0.0)
        self.meet(ref[at + 2 : at + 3, :])


def strip(rows_value, others, flags, outs, out_rows):
    row_top = row_mass = None
    for other, flag, out in zip(others, flags, outs):
        sims = tile(rows_value, other)
        weights = jnp.exp2(sims * TO_EXP2)
        out.add(jnp.max(sims, axis=0, keepdims=True), jnp.sum(weights, axis=0, keepdims=True), flag[:, : sims.shape[1]])
        top = jnp.where(flag[:, :LANES], lane_groups(sims, jnp.maximum), LOW)
        mass = jnp.where(flag[:, :LANES], lane_groups(weights, jnp.add), 0.0)
        row_top = top if row_top is None else jnp.maximum(row_top, top)
        row_mass = mass if row_mass is None else row_mass + mass
    out_rows.append((rows_done(row_top, jnp.max), rows_done(row_mass, jnp.sum)))


def whole(parts):
    return [jnp.concatenate([part[which] for part in parts], axis=1) for which in range(2)]


def near_kernel(unit_ref, near_ref, out_ref):
    unit = rows_of(unit_ref)
    rows = unit.shape[0]
    flag = tail_of(unit_ref)[1] == tail_of(near_ref)[1]
    mine, near, parts = Columns(rows), Columns(rows), []
    for at in range(0, rows, STRIP):
        sims = tile(unit_ref[at : at + STRIP, :], unit)
        row = lax.broadcasted_iota(jnp.int32, sims.shape, 0) + at
        same = row == lax.broadcasted_iota(jnp.int32, sims.shape, 1)
        weights = jnp.where(same, 0.0, jnp.exp2(sims * TO_EXP2))
        sims = jnp.where(same, LOW, sims)
        mine.add(jnp.max(sims, axis=0, keepdims=True), jnp.sum(weights, axis=0, keepdims=True))
        strip(near_ref[at : at + STRIP, :], (unit,), (flag,), (mine,), parts)
    near.add(*whole(parts))
    mine.store(out_ref, 0)
    near.store(out_ref, 2)


def far_kernel(
    far_ref, unit_ref, other_ref, near_ref, near_x_ref, back_ref, stats_ref,
    mine_ref, swap_ref, near_out_ref, far_out_ref, back_out_ref,
):
    unit, other = rows_of(unit_ref), rows_of(other_ref)
    rows, width = unit.shape
    second = this_core() == 1
    mine, across, near, near_x = columns = [Columns(rows, width) for _ in range(4)]
    theirs, beyond, last = Columns(rows, width), Columns(rows, width), Columns(rows)
    blocks = (unit, other, rows_of(near_ref), rows_of(near_x_ref))
    tails = [tail_of(ref) for ref in (unit_ref, other_ref, near_ref, near_x_ref)]
    far_tail, back_tail = tail_of(far_ref), tail_of(back_ref)
    last_block = jnp.where(second, other, rows_of(back_ref))
    last_flag = jnp.where(second, tails[0][1], far_tail[1]) == jnp.where(second, tails[1][1], back_tail[1])
    flags = [tag == far_tail[1] for _, tag in tails]
    near_flag = tails[1][1] == tails[2][1]
    far, extra, back_by = [], [], []
    for at in range(0, rows, STRIP):
        far_rows = far_ref[at : at + STRIP, :]
        strip(far_rows, blocks, flags, columns, far)
        strip(near_ref[at : at + STRIP, :], (other,), (near_flag,), (across,), back_by)
        last_rows = jnp.where(second, unit_ref[at : at + STRIP, :], far_rows)
        strip(last_rows, (last_block,), (last_flag,), (last,), extra)
    mine.meet(tails[0][0])
    for (total, tag), owner in zip(tails[:2], (mine, across)):
        near.meet(total, tag == tails[2][1])
        owner.meet(tails[2][0], tag == tails[2][1])
    for (total, _), flag, owner in zip(tails, flags, columns):
        theirs.meet(total, flag)
        owner.meet(far_tail[0], flag)
    on = jnp.logical_and(last_flag, second)
    off = jnp.logical_and(last_flag, jnp.logical_not(second))
    across.meet(tails[0][0], on)
    mine.meet(tails[1][0], on)
    beyond.meet(far_tail[0], off)
    theirs.meet(back_tail[0], off)
    extra = whole(extra)
    theirs.add(*whole(far))
    theirs.add(*extra, off[:, :rows])
    mine.add(*extra, on[:, :rows])
    across.add(last.top, last.mass, on[:, :rows])
    beyond.add(last.top, last.mass, off[:, :rows])
    near.add(*whole(back_by))
    mine.load(stats_ref, 0)
    near.load(stats_ref, 2)
    mine.store(mine_ref, 0)
    across.store(swap_ref, 0)
    near_x.store(swap_ref, 3)
    near.store(near_out_ref, 0)
    theirs.store(far_out_ref, 0)
    beyond.store(back_out_ref, 0)


def sum_kernel(*refs, rows, places):
    found = Columns(rows, refs[-1].shape[1])
    for ref, place in zip(refs, places):
        found.receive(ref, place)
    found.store(refs[-1], 0)


def final_kernel(unit_ref, most_ref, back_ref, top_ref, log_ref, cos_ref):
    unit = rows_of(unit_ref)
    rows, width = unit.shape
    mine = Columns(rows, width)
    for ref in (most_ref, back_ref):
        mine.receive(ref, 0)
    top_ref[...] = mine.top
    log_ref[...] = jnp.log(mine.mass)
    mean = jnp.sum(mine.total * mine.total, axis=1, keepdims=True) / width
    centre = mine.total * (lax.rsqrt(mean + 1e-06) / math.sqrt(width))
    parts = [part.astype(F32) for part in parts_of(centre)]
    cosines = tile(jnp.concatenate(parts + [jnp.zeros((5, width), F32)]).astype(BF16), unit)
    cos_ref[...] = cosines[0:1, :] + (cosines[1:2, :] + cosines[2:3, :])


def per_device(embeddings, cluster_ids):
    rows, width = embeddings.shape
    block = unit_block(embeddings, cluster_ids)

    near = blocks_moved(block, 2)
    far = blocks_moved(block, -4)
    back = blocks_moved(near, 1, core=1)
    near_x = cores_swapped(near)
    other = cores_swapped(after(block, near))
    stats = call(near_kernel, shape(4, rows), block, near)
    mine, swap, near_out, far_out, back_out = call(
        far_kernel,
        [shape(3, width), shape(6, width), shape(3, width), shape(3, width), shape(3, width)],
        far, block, other, near, near_x, back, stats,
    )
    swap_in = cores_swapped(swap)
    far_in = blocks_moved(far_out, 4)
    near_all = call(functools.partial(sum_kernel, rows=rows, places=(0, 3)), shape(3, width), near_out, swap_in)
    near_in = blocks_moved(near_all, -2)
    back_in = blocks_moved(after(back_out, near_all), -3, core=0)
    most = call(functools.partial(sum_kernel, rows=rows, places=(0, 0, 0, 0)), shape(3, width), mine, swap_in, far_in, near_in)
    outs = call(final_kernel, [shape(1, rows)] * 3, block, most, back_in)
    return tuple(out.reshape(rows) for out in outs)


def solution(mesh):
    in_specs = (P(AXES, None), P(AXES))
    out_specs = (P(AXES), P(AXES), P(AXES))
    return jax.shard_map(per_device, mesh=mesh, in_specs=in_specs, out_specs=out_specs, check_vma=False)
```

```python
import functools
import math

import jax
import jax.numpy as jnp
from jax import lax
from jax.experimental import pallas as pl
from jax.experimental.pallas import tpu as pltpu
from jax.sharding import PartitionSpec as P

TAU = 0.05
LOW = -2.0
TO_EXP2 = math.log2(math.e) / TAU
AXES = ("shard", "grp")
VMEM = pl.BlockSpec(memory_space=pltpu.VMEM)
F32 = jnp.float32
BF16 = jnp.bfloat16
LANES = 128
TAIL = 16
STRIP = 256


def shape(*dims, dtype=F32):
    return jax.ShapeDtypeStruct(dims, dtype)


def call(kernel, outs, *args, limit=16):
    single = not isinstance(outs, (list, tuple))
    size = sum(a.size * a.dtype.itemsize for a in args)
    return pl.pallas_call(
        kernel,
        out_shape=outs,
        in_specs=[VMEM] * len(args),
        out_specs=VMEM if single else [VMEM] * len(outs),
        compiler_params=pltpu.CompilerParams(vmem_limit_bytes=limit << 20),
        cost_estimate=pl.CostEstimate(flops=0, bytes_accessed=size, transcendentals=0),
    )(*args)


def blocks_moved(value, steps, core=None):
    count = lax.axis_size(AXES)
    pairs = [(i, i + steps) for i in range(count) if core in (None, i % 2) and 0 <= i + steps < count]
    return lax.ppermute(value, AXES, pairs)


def cores_swapped(value):
    return lax.ppermute(value, AXES, [(i, i ^ 1) for i in range(lax.axis_size(AXES))])


def after(value, *others):
    return lax.optimization_barrier((value, *others))[0]


def parts_of(value):
    high = value.astype(BF16)
    rest = value - high.astype(F32)
    middle = rest.astype(BF16)
    return high, middle, (rest - middle.astype(F32)).astype(BF16)


def unit_kernel(id_ref, emb_ref, block_ref):
    rows, width = emb_ref.shape
    total = jnp.zeros((8, width), F32)
    for at in range(0, rows, STRIP // 2):
        strip_rows = slice(at, at + STRIP // 2)
        floats = emb_ref[strip_rows, :].astype(F32)
        mean = jnp.sum(floats * floats, axis=1, keepdims=True) / width
        unit = (floats * (lax.rsqrt(mean + 1e-06) / math.sqrt(width))).astype(BF16)
        block_ref[strip_rows, :] = unit
        total += jnp.dot(jnp.ones((8, STRIP // 2), BF16), unit, preferred_element_type=F32)
    parts = [part.astype(F32) for part in parts_of(total[0:1, :])]
    tag = jnp.full((1, width), (id_ref[0] + 1).astype(F32))
    block_ref[rows:, :] = jnp.concatenate(parts + [tag, jnp.zeros((TAIL - 4, width), F32)]).astype(BF16)


def unit_block(embeddings, cluster_ids):
    rows, width = embeddings.shape
    return pl.pallas_call(
        unit_kernel,
        out_shape=shape(rows + TAIL, width, dtype=BF16),
        in_specs=[pl.BlockSpec(memory_space=pltpu.SMEM), VMEM],
        out_specs=VMEM,
        compiler_params=pltpu.CompilerParams(vmem_limit_bytes=16 << 20),
    )(cluster_ids, embeddings)


def this_core():
    return lax.rem(lax.axis_index("grp"), 2)


def rows_of(ref):
    return ref[: ref.shape[0] - TAIL, :]


def tail_of(ref):
    tail = ref[ref.shape[0] - TAIL :, :].astype(F32)
    return tail[0:1, :] + (tail[1:2, :] + tail[2:3, :]), tail[3:4, :]


def tile(left, right):
    return lax.dot_general(left, right, (((1,), (1,)), ((), ())), preferred_element_type=F32)


def lane_groups(value, combine):
    return functools.reduce(combine, [value[:, at : at + 128] for at in range(0, value.shape[1], 128)])


def rows_done(value, combine):
    return combine(value.T, axis=0, keepdims=True)


class Columns:
    def __init__(self, rows, width=0):
        self.top = jnp.full((1, rows), LOW, F32)
        self.mass = jnp.zeros((1, rows), F32)
        self.total = jnp.zeros((1, width), F32)

    def add(self, top, mass, flag=None):
        if flag is not None:
            top = jnp.where(flag, top, LOW)
            mass = jnp.where(flag, mass, 0.0)
        self.top = jnp.maximum(self.top, top)
        self.mass = self.mass + mass

    def meet(self, total, flag=None):
        self.total = self.total + (total if flag is None else jnp.where(flag, total, 0.0))

    def load(self, ref, at):
        rows = self.top.shape[1]
        self.add(ref[at : at + 1, :rows], ref[at + 1 : at + 2, :rows])

    def store(self, ref, at):
        rows = self.top.shape[1]
        ref[at : at + 1, :rows] = self.top
        ref[at + 1 : at + 2, :rows] = self.mass
        if self.total.size:
            ref[at : at + 2, rows:] = jnp.zeros((2, ref.shape[1] - rows), F32)
            ref[at + 2 : at + 3, :] = self.total

    def receive(self, ref, at):
        rows = self.top.shape[1]
        mass = ref[at + 1 : at + 2, :rows]
        self.add(ref[at : at + 1, :rows], mass, mass > 0.0)
        self.meet(ref[at + 2 : at + 3, :])


def strip(rows_value, others, flags, outs, out_rows):
    row_top = row_mass = None
    for other, flag, out in zip(others, flags, outs):
        sims = tile(rows_value, other)
        weights = jnp.exp2(sims * TO_EXP2)
        out.add(jnp.max(sims, axis=0, keepdims=True), jnp.sum(weights, axis=0, keepdims=True), flag[:, : sims.shape[1]])
        top = jnp.where(flag[:, :LANES], lane_groups(sims, jnp.maximum), LOW)
        mass = jnp.where(flag[:, :LANES], lane_groups(weights, jnp.add), 0.0)
        row_top = top if row_top is None else jnp.maximum(row_top, top)
        row_mass = mass if row_mass is None else row_mass + mass
    out_rows.append((rows_done(row_top, jnp.max), rows_done(row_mass, jnp.sum)))


def whole(parts):
    return [jnp.concatenate([part[which] for part in parts], axis=1) for which in range(2)]


def near_kernel(unit_ref, near_ref, out_ref):
    unit = rows_of(unit_ref)
    rows = unit.shape[0]
    flag = tail_of(unit_ref)[1] == tail_of(near_ref)[1]
    mine, near, parts = Columns(rows), Columns(rows), []
    for at in range(0, rows, STRIP):
        sims = tile(unit_ref[at : at + STRIP, :], unit)
        row = lax.broadcasted_iota(jnp.int32, sims.shape, 0) + at
        same = row == lax.broadcasted_iota(jnp.int32, sims.shape, 1)
        weights = jnp.where(same, 0.0, jnp.exp2(sims * TO_EXP2))
        sims = jnp.where(same, LOW, sims)
        mine.add(jnp.max(sims, axis=0, keepdims=True), jnp.sum(weights, axis=0, keepdims=True))
        strip(near_ref[at : at + STRIP, :], (unit,), (flag,), (mine,), parts)
    near.add(*whole(parts))
    mine.store(out_ref, 0)
    near.store(out_ref, 2)


def far_kernel(
    far_ref, unit_ref, other_ref, near_ref, near_x_ref, back_ref, stats_ref,
    mine_ref, swap_ref, near_out_ref, far_out_ref, back_out_ref,
):
    unit, other = rows_of(unit_ref), rows_of(other_ref)
    rows, width = unit.shape
    second = this_core() == 1
    mine, across, near, near_x = columns = [Columns(rows, width) for _ in range(4)]
    theirs, beyond, last = Columns(rows, width), Columns(rows, width), Columns(rows)
    blocks = (unit, other, rows_of(near_ref), rows_of(near_x_ref))
    tails = [tail_of(ref) for ref in (unit_ref, other_ref, near_ref, near_x_ref)]
    far_tail, back_tail = tail_of(far_ref), tail_of(back_ref)
    last_block = jnp.where(second, other, rows_of(back_ref))
    last_flag = jnp.where(second, tails[0][1], far_tail[1]) == jnp.where(second, tails[1][1], back_tail[1])
    flags = [tag == far_tail[1] for _, tag in tails]
    near_flag = tails[1][1] == tails[2][1]
    def far_tiles():
        found, parts = [Columns(rows) for _ in blocks], []
        for at in range(0, rows, STRIP):
            strip(far_ref[at : at + STRIP, :], blocks, flags, found, parts)
        return [value for column in found for value in (column.top, column.mass)] + whole(parts)

    def near_tiles():
        found, parts = Columns(rows), []
        for at in range(0, rows, STRIP):
            strip(near_ref[at : at + STRIP, :], (other,), (near_flag,), (found,), parts)
        return [found.top, found.mass] + whole(parts)

    def last_tiles():
        found, parts = Columns(rows), []
        for at in range(0, rows, STRIP):
            last_rows = jnp.where(second, unit_ref[at : at + STRIP, :], far_ref[at : at + STRIP, :])
            strip(last_rows, (last_block,), (last_flag,), (found,), parts)
        return [found.top, found.mass] + whole(parts)

    def where_met(some, tiles, pairs):
        met = jnp.max(functools.reduce(jnp.maximum, [jnp.where(flag[:, :LANES], 1.0, 0.0) for flag in some])) > 0.5
        nothing = [jnp.full((1, rows), LOW, F32), jnp.zeros((1, rows), F32)] * pairs
        return lax.cond(met, tiles, lambda: nothing)

    found = where_met(flags, far_tiles, 5)
    for at, column in enumerate(columns):
        column.add(found[2 * at], found[2 * at + 1])
    far = found[8:]
    found = where_met((near_flag,), near_tiles, 2)
    across.add(found[0], found[1])
    back_by = found[2:]
    found = where_met((last_flag,), last_tiles, 2)
    last.add(found[0], found[1])
    extra = found[2:]
    mine.meet(tails[0][0])
    for (total, tag), owner in zip(tails[:2], (mine, across)):
        near.meet(total, tag == tails[2][1])
        owner.meet(tails[2][0], tag == tails[2][1])
    for (total, _), flag, owner in zip(tails, flags, columns):
        theirs.meet(total, flag)
        owner.meet(far_tail[0], flag)
    on = jnp.logical_and(last_flag, second)
    off = jnp.logical_and(last_flag, jnp.logical_not(second))
    across.meet(tails[0][0], on)
    mine.meet(tails[1][0], on)
    beyond.meet(far_tail[0], off)
    theirs.meet(back_tail[0], off)
    theirs.add(*far)
    theirs.add(*extra, off[:, :rows])
    mine.add(*extra, on[:, :rows])
    across.add(last.top, last.mass, on[:, :rows])
    beyond.add(last.top, last.mass, off[:, :rows])
    near.add(*back_by)
    mine.load(stats_ref, 0)
    near.load(stats_ref, 2)
    mine.store(mine_ref, 0)
    across.store(swap_ref, 0)
    near_x.store(swap_ref, 3)
    near.store(near_out_ref, 0)
    theirs.store(far_out_ref, 0)
    beyond.store(back_out_ref, 0)


def sum_kernel(*refs, rows, places):
    found = Columns(rows, refs[-1].shape[1])
    for ref, place in zip(refs, places):
        found.receive(ref, place)
    found.store(refs[-1], 0)


def final_kernel(unit_ref, most_ref, back_ref, top_ref, log_ref, cos_ref):
    unit = rows_of(unit_ref)
    rows, width = unit.shape
    mine = Columns(rows, width)
    for ref in (most_ref, back_ref):
        mine.receive(ref, 0)
    top_ref[...] = mine.top
    log_ref[...] = jnp.log(mine.mass)
    mean = jnp.sum(mine.total * mine.total, axis=1, keepdims=True) / width
    centre = mine.total * (lax.rsqrt(mean + 1e-06) / math.sqrt(width))
    parts = [part.astype(F32) for part in parts_of(centre)]
    cosines = tile(jnp.concatenate(parts + [jnp.zeros((5, width), F32)]).astype(BF16), unit)
    cos_ref[...] = cosines[0:1, :] + (cosines[1:2, :] + cosines[2:3, :])


def per_device(embeddings, cluster_ids):
    rows, width = embeddings.shape
    block = unit_block(embeddings, cluster_ids)

    near = blocks_moved(block, 2)
    far = blocks_moved(block, -4)
    back = blocks_moved(near, 1, core=1)
    near_x = cores_swapped(near)
    other = cores_swapped(after(block, near))
    stats = call(near_kernel, shape(4, rows), block, near)
    mine, swap, near_out, far_out, back_out = call(
        far_kernel,
        [shape(3, width), shape(6, width), shape(3, width), shape(3, width), shape(3, width)],
        far, block, other, near, near_x, back, stats,
    )
    swap_in = cores_swapped(swap)
    far_in = blocks_moved(far_out, 4)
    near_all = call(functools.partial(sum_kernel, rows=rows, places=(0, 3)), shape(3, width), near_out, swap_in)
    near_in = blocks_moved(near_all, -2)
    back_in = blocks_moved(after(back_out, near_all), -3, core=0)
    most = call(functools.partial(sum_kernel, rows=rows, places=(0, 0, 0, 0)), shape(3, width), mine, swap_in, far_in, near_in)
    outs = call(final_kernel, [shape(1, rows)] * 3, block, most, back_in)
    return tuple(out.reshape(rows) for out in outs)


def solution(mesh):
    in_specs = (P(AXES, None), P(AXES))
    out_specs = (P(AXES), P(AXES), P(AXES))
    return jax.shard_map(per_device, mesh=mesh, in_specs=in_specs, out_specs=out_specs, check_vma=False)
```

```python
import functools
import math

import jax
import jax.numpy as jnp
from jax import lax
from jax.experimental import pallas as pl
from jax.experimental.pallas import tpu as pltpu
from jax.sharding import PartitionSpec as P

TAU = 0.05
LOW = -2.0
TO_EXP2 = math.log2(math.e) / TAU
AXES = ("shard", "grp")
VMEM = pl.BlockSpec(memory_space=pltpu.VMEM)
F32 = jnp.float32
BF16 = jnp.bfloat16
LANES = 128
TAIL = 16
STRIP = 256


def shape(*dims, dtype=F32):
    return jax.ShapeDtypeStruct(dims, dtype)


def call(kernel, outs, *args, limit=16):
    single = not isinstance(outs, (list, tuple))
    size = sum(a.size * a.dtype.itemsize for a in args)
    return pl.pallas_call(
        kernel,
        out_shape=outs,
        in_specs=[VMEM] * len(args),
        out_specs=VMEM if single else [VMEM] * len(outs),
        compiler_params=pltpu.CompilerParams(vmem_limit_bytes=limit << 20),
        cost_estimate=pl.CostEstimate(flops=0, bytes_accessed=size, transcendentals=0),
    )(*args)


def blocks_moved(value, steps, core=None):
    count = lax.axis_size(AXES)
    pairs = [(i, i + steps) for i in range(count) if core in (None, i % 2) and 0 <= i + steps < count]
    return lax.ppermute(value, AXES, pairs)


def cores_swapped(value):
    return lax.ppermute(value, AXES, [(i, i ^ 1) for i in range(lax.axis_size(AXES))])


def after(value, *others):
    return lax.optimization_barrier((value, *others))[0]


def parts_of(value):
    high = value.astype(BF16)
    rest = value - high.astype(F32)
    middle = rest.astype(BF16)
    return high, middle, (rest - middle.astype(F32)).astype(BF16)


def unit_kernel(id_ref, emb_ref, block_ref):
    rows, width = emb_ref.shape
    total = jnp.zeros((8, width), F32)
    for at in range(0, rows, STRIP // 2):
        strip_rows = slice(at, at + STRIP // 2)
        floats = emb_ref[strip_rows, :].astype(F32)
        mean = jnp.sum(floats * floats, axis=1, keepdims=True) / width
        unit = (floats * (lax.rsqrt(mean + 1e-06) / math.sqrt(width))).astype(BF16)
        block_ref[strip_rows, :] = unit
        total += jnp.dot(jnp.ones((8, STRIP // 2), BF16), unit, preferred_element_type=F32)
    parts = [part.astype(F32) for part in parts_of(total[0:1, :])]
    tag = jnp.full((1, width), (id_ref[0] + 1).astype(F32))
    block_ref[rows:, :] = jnp.concatenate(parts + [tag, jnp.zeros((TAIL - 4, width), F32)]).astype(BF16)


def unit_block(embeddings, cluster_ids):
    rows, width = embeddings.shape
    return pl.pallas_call(
        unit_kernel,
        out_shape=shape(rows + TAIL, width, dtype=BF16),
        in_specs=[pl.BlockSpec(memory_space=pltpu.SMEM), VMEM],
        out_specs=VMEM,
        compiler_params=pltpu.CompilerParams(vmem_limit_bytes=16 << 20),
    )(cluster_ids, embeddings)


def this_core():
    return lax.rem(lax.axis_index("grp"), 2)


def rows_of(ref):
    return ref[: ref.shape[0] - TAIL, :]


def tail_of(ref):
    tail = ref[ref.shape[0] - TAIL :, :].astype(F32)
    return tail[0:1, :] + (tail[1:2, :] + tail[2:3, :]), tail[3:4, :]


def tile(left, right):
    return lax.dot_general(left, right, (((1,), (1,)), ((), ())), preferred_element_type=F32)


def lane_groups(value, combine):
    return functools.reduce(combine, [value[:, at : at + 128] for at in range(0, value.shape[1], 128)])


def rows_done(value, combine):
    return combine(value.T, axis=0, keepdims=True)


class Columns:
    def __init__(self, rows, width=0):
        self.top = jnp.full((1, rows), LOW, F32)
        self.mass = jnp.zeros((1, rows), F32)
        self.total = jnp.zeros((1, width), F32)

    def add(self, top, mass, flag=None):
        if flag is not None:
            top = jnp.where(flag, top, LOW)
            mass = jnp.where(flag, mass, 0.0)
        self.top = jnp.maximum(self.top, top)
        self.mass = self.mass + mass

    def meet(self, total, flag=None):
        self.total = self.total + (total if flag is None else jnp.where(flag, total, 0.0))

    def load(self, ref, at):
        rows = self.top.shape[1]
        self.add(ref[at : at + 1, :rows], ref[at + 1 : at + 2, :rows])

    def store(self, ref, at):
        rows = self.top.shape[1]
        ref[at : at + 1, :rows] = self.top
        ref[at + 1 : at + 2, :rows] = self.mass
        if self.total.size:
            ref[at : at + 2, rows:] = jnp.zeros((2, ref.shape[1] - rows), F32)
            ref[at + 2 : at + 3, :] = self.total

    def receive(self, ref, at):
        rows = self.top.shape[1]
        mass = ref[at + 1 : at + 2, :rows]
        self.add(ref[at : at + 1, :rows], mass, mass > 0.0)
        self.meet(ref[at + 2 : at + 3, :])


def strip(rows_value, others, flags, outs, out_rows):
    row_top = row_mass = None
    for other, flag, out in zip(others, flags, outs):
        sims = tile(rows_value, other)
        weights = jnp.exp2(sims * TO_EXP2)
        out.add(jnp.max(sims, axis=0, keepdims=True), jnp.sum(weights, axis=0, keepdims=True), flag[:, : sims.shape[1]])
        top = jnp.where(flag[:, :LANES], lane_groups(sims, jnp.maximum), LOW)
        mass = jnp.where(flag[:, :LANES], lane_groups(weights, jnp.add), 0.0)
        row_top = top if row_top is None else jnp.maximum(row_top, top)
        row_mass = mass if row_mass is None else row_mass + mass
    out_rows.append((rows_done(row_top, jnp.max), rows_done(row_mass, jnp.sum)))


def whole(parts):
    return [jnp.concatenate([part[which] for part in parts], axis=1) for which in range(2)]


def near_kernel(unit_ref, near_ref, out_ref):
    unit = rows_of(unit_ref)
    rows = unit.shape[0]
    flag = tail_of(unit_ref)[1] == tail_of(near_ref)[1]
    mine, near, parts = Columns(rows), Columns(rows), []
    for at in range(0, rows, STRIP):
        sims = tile(unit_ref[at : at + STRIP, :], unit)
        row = lax.broadcasted_iota(jnp.int32, sims.shape, 0) + at
        same = row == lax.broadcasted_iota(jnp.int32, sims.shape, 1)
        weights = jnp.where(same, 0.0, jnp.exp2(sims * TO_EXP2))
        sims = jnp.where(same, LOW, sims)
        mine.add(jnp.max(sims, axis=0, keepdims=True), jnp.sum(weights, axis=0, keepdims=True))
        strip(near_ref[at : at + STRIP, :], (unit,), (flag,), (mine,), parts)
    near.add(*whole(parts))
    mine.store(out_ref, 0)
    near.store(out_ref, 2)


def far_kernel(
    far_ref, unit_ref, other_ref, near_ref, near_x_ref, back_ref, stats_ref,
    mine_ref, swap_ref, near_out_ref, far_out_ref, back_out_ref,
):
    unit, other = rows_of(unit_ref), rows_of(other_ref)
    rows, width = unit.shape
    second = this_core() == 1
    mine, across, near, near_x = columns = [Columns(rows, width) for _ in range(4)]
    theirs, beyond, last = Columns(rows, width), Columns(rows, width), Columns(rows)
    blocks = (unit, other, rows_of(near_ref), rows_of(near_x_ref))
    tails = [tail_of(ref) for ref in (unit_ref, other_ref, near_ref, near_x_ref)]
    far_tail, back_tail = tail_of(far_ref), tail_of(back_ref)
    last_block = jnp.where(second, other, rows_of(back_ref))
    last_flag = jnp.where(second, tails[0][1], far_tail[1]) == jnp.where(second, tails[1][1], back_tail[1])
    flags = [tag == far_tail[1] for _, tag in tails]
    near_flag = tails[1][1] == tails[2][1]
    def far_tiles(pair):
        found, parts = [Columns(rows) for _ in blocks[pair]], []
        for at in range(0, rows, STRIP):
            strip(far_ref[at : at + STRIP, :], blocks[pair], flags[pair], found, parts)
        return [value for column in found for value in (column.top, column.mass)] + whole(parts)

    def near_tiles():
        found, parts = Columns(rows), []
        for at in range(0, rows, STRIP):
            strip(near_ref[at : at + STRIP, :], (other,), (near_flag,), (found,), parts)
        return [found.top, found.mass] + whole(parts)

    def last_tiles():
        found, parts = Columns(rows), []
        for at in range(0, rows, STRIP):
            last_rows = jnp.where(second, unit_ref[at : at + STRIP, :], far_ref[at : at + STRIP, :])
            strip(last_rows, (last_block,), (last_flag,), (found,), parts)
        return [found.top, found.mass] + whole(parts)

    def where_met(some, tiles, pairs):
        met = jnp.max(functools.reduce(jnp.maximum, [jnp.where(flag[:, :LANES], 1.0, 0.0) for flag in some])) > 0.5
        nothing = [jnp.full((1, rows), LOW, F32), jnp.zeros((1, rows), F32)] * pairs
        return lax.cond(met, tiles, lambda: nothing)

    for pair in (slice(0, 2), slice(2, 4)):
        found = where_met(flags[pair], functools.partial(far_tiles, pair), 3)
        for at, column in enumerate((*columns[pair], theirs)):
            column.add(found[2 * at], found[2 * at + 1])
    found = where_met((near_flag,), near_tiles, 2)
    across.add(found[0], found[1])
    back_by = found[2:]
    found = where_met((last_flag,), last_tiles, 2)
    last.add(found[0], found[1])
    extra = found[2:]
    mine.meet(tails[0][0])
    for (total, tag), owner in zip(tails[:2], (mine, across)):
        near.meet(total, tag == tails[2][1])
        owner.meet(tails[2][0], tag == tails[2][1])
    for (total, _), flag, owner in zip(tails, flags, columns):
        theirs.meet(total, flag)
        owner.meet(far_tail[0], flag)
    on = jnp.logical_and(last_flag, second)
    off = jnp.logical_and(last_flag, jnp.logical_not(second))
    across.meet(tails[0][0], on)
    mine.meet(tails[1][0], on)
    beyond.meet(far_tail[0], off)
    theirs.meet(back_tail[0], off)
    theirs.add(*extra, off[:, :rows])
    mine.add(*extra, on[:, :rows])
    across.add(last.top, last.mass, on[:, :rows])
    beyond.add(last.top, last.mass, off[:, :rows])
    near.add(*back_by)
    mine.load(stats_ref, 0)
    near.load(stats_ref, 2)
    mine.store(mine_ref, 0)
    across.store(swap_ref, 0)
    near_x.store(swap_ref, 3)
    near.store(near_out_ref, 0)
    theirs.store(far_out_ref, 0)
    beyond.store(back_out_ref, 0)


def sum_kernel(*refs, rows, places):
    found = Columns(rows, refs[-1].shape[1])
    for ref, place in zip(refs, places):
        found.receive(ref, place)
    found.store(refs[-1], 0)


def final_kernel(unit_ref, most_ref, back_ref, top_ref, log_ref, cos_ref):
    unit = rows_of(unit_ref)
    rows, width = unit.shape
    mine = Columns(rows, width)
    for ref in (most_ref, back_ref):
        mine.receive(ref, 0)
    top_ref[...] = mine.top
    log_ref[...] = jnp.log(mine.mass)
    mean = jnp.sum(mine.total * mine.total, axis=1, keepdims=True) / width
    centre = mine.total * (lax.rsqrt(mean + 1e-06) / math.sqrt(width))
    parts = [part.astype(F32) for part in parts_of(centre)]
    cosines = tile(jnp.concatenate(parts + [jnp.zeros((5, width), F32)]).astype(BF16), unit)
    cos_ref[...] = cosines[0:1, :] + (cosines[1:2, :] + cosines[2:3, :])


def per_device(embeddings, cluster_ids):
    rows, width = embeddings.shape
    block = unit_block(embeddings, cluster_ids)

    near = blocks_moved(block, 2)
    far = blocks_moved(block, -4)
    back = blocks_moved(near, 1, core=1)
    near_x = cores_swapped(near)
    other = cores_swapped(after(block, near))
    stats = call(near_kernel, shape(4, rows), block, near)
    mine, swap, near_out, far_out, back_out = call(
        far_kernel,
        [shape(3, width), shape(6, width), shape(3, width), shape(3, width), shape(3, width)],
        far, block, other, near, near_x, back, stats,
    )
    swap_in = cores_swapped(swap)
    far_in = blocks_moved(far_out, 4)
    near_all = call(functools.partial(sum_kernel, rows=rows, places=(0, 3)), shape(3, width), near_out, swap_in)
    near_in = blocks_moved(near_all, -2)
    back_in = blocks_moved(after(back_out, near_all), -3, core=0)
    most = call(functools.partial(sum_kernel, rows=rows, places=(0, 0, 0, 0)), shape(3, width), mine, swap_in, far_in, near_in)
    outs = call(final_kernel, [shape(1, rows)] * 3, block, most, back_in)
    return tuple(out.reshape(rows) for out in outs)


def solution(mesh):
    in_specs = (P(AXES, None), P(AXES))
    out_specs = (P(AXES), P(AXES), P(AXES))
    return jax.shard_map(per_device, mesh=mesh, in_specs=in_specs, out_specs=out_specs, check_vma=False)
```
